32 devices in a mesh: dp: 32 (over z, y, x, core).
Axes of the slice: x: 2, y: 2, z: 4, core: 2. Of those that a mesh axis runs over, the one named last changes fastest.
Arguments:
- tokens: bfloat16 [16384, 768], P('dp'), may hold values from -6 to 6
- cotangent: bfloat16 [16384, 768], P('dp'), may hold values from -6 to 6
- seq_len: int32 [32], P('dp'), may hold values from 64 to 512, as said below
- ln1_gain: bfloat16 [2, 768], P(None, 'dp'), may hold values from 0.5 to 1.5
- ln1_bias: bfloat16 [2, 768], P(None, 'dp'), may hold values from -3 to 3
- qkv_weight: bfloat16 [2, 768, 2304], P(None, 'dp'), may hold values from -0.21875 to 0.21875
- qv_bias: bfloat16 [2, 1536], P(None, 'dp'), may hold values from -3 to 3
- out_weight: bfloat16 [2, 768, 768], P(None, 'dp'), may hold values from -1.75 to 1.75
- out_bias: bfloat16 [2, 768], P(None, 'dp'), may hold values from -3 to 3
- ln2_gain: bfloat16 [2, 768], P(None, 'dp'), may hold values from 0.5 to 1.5
- ln2_bias: bfloat16 [2, 768], P(None, 'dp'), may hold values from -3 to 3
- fc_weight: bfloat16 [2, 768, 3072], P(None, 'dp'), may hold values from -0.21875 to 0.21875
- fc_bias: bfloat16 [2, 3072], P(None, 'dp'), may hold values from -3 to 3
- proj_weight: bfloat16 [2, 3072, 768], P(None, 'dp'), may hold values from -0.109375 to 0.109375
- proj_bias: bfloat16 [2, 768], P(None, 'dp'), may hold values from -3 to 3
Outputs:
- output: bfloat16 [16384, 768], P('dp')
- tokens_grad: bfloat16 [16384, 768], P('dp')
- ln1_gain_grad: float32 [2, 768], P(None, 'dp')
- ln1_bias_grad: float32 [2, 768], P(None, 'dp')
- qkv_weight_grad: float32 [2, 768, 2304], P(None, 'dp')
- qv_bias_grad: float32 [2, 1536], P(None, 'dp')
- out_weight_grad: float32 [2, 768, 768], P(None, 'dp')
- out_bias_grad: float32 [2, 768], P(None, 'dp')
- ln2_gain_grad: float32 [2, 768], P(None, 'dp')
- ln2_bias_grad: float32 [2, 768], P(None, 'dp')
- fc_weight_grad: float32 [2, 768, 3072], P(None, 'dp')
- fc_bias_grad: float32 [2, 3072], P(None, 'dp')
- proj_weight_grad: float32 [2, 3072, 768], P(None, 'dp')
- proj_bias_grad: float32 [2, 768], P(None, 'dp')
The draws below stay inside these ranges and needn't reach their ends.
Inputs may be any that keep to these rules, and one draw needn't show every extreme that they name: `seq_len`: each sequence has 64 to 512 live tokens; some sequence has exactly 512.
All inputs are finite; a program needn't handle non-finite values.
Results may differ from the reference program's by a relative error of at most 0.015.
Values may be sent and summed in bfloat16 or wider, within the bound.
A program may use at most 320 MiB of HBM per device.

```python
import math
import jax
import jax.numpy as jnp
from jax import lax

D = 768
H = 12
HD = 64
FF = 3072
SEQ = 512
LAYERS = 2
SLOTS = 32
TOKENS = 16384


def draw_seq_len(key, part):
    first, second = jax.random.split(jax.random.fold_in(key, 17))
    lengths = jax.random.randint(first, (SLOTS,), SEQ // 8, SEQ + 1)
    where_full = jax.random.randint(second, (), 0, SLOTS)
    return lengths.at[where_full].set(SEQ).astype(jnp.int32)


def steps_of(rng, shape, cuts, least, high):
    level = 1.0
    for axis_at, parts in cuts:
        draws = jax.random.uniform(jax.random.fold_in(jax.random.fold_in(rng, 6), axis_at), (parts,), jnp.float32, least / len(cuts), high / len(cuts))
        level = level * jnp.repeat(jnp.exp(draws), shape[axis_at] // parts).reshape((-1,) + (1,) * (len(shape) - 1 - axis_at))
    return level


def normal_values(stream_key, shape, width, most, cuts=(), kind=jnp.bfloat16):
    loudness = steps_of(stream_key, shape, cuts, -0.22, 0.18) if cuts else 1.0
    values = jax.random.normal(stream_key, shape, jnp.float32) * width * loudness
    return jnp.minimum(jnp.maximum(values, -most), most).astype(kind)


def setup_inputs(seed: int = 0) -> dict:
    seeds = jax.random.split(jax.random.key(seed), 16)
    tokens = normal_values(seeds[0], (TOKENS, D), 1.0, 6.0, ((0, 32),))
    cotangent = normal_values(seeds[1], (TOKENS, D), 1.0, 6.0, ((0, 32),))
    seq_len = draw_seq_len(jax.random.fold_in(seeds[15], 71), 0)
    ln1_gain = jnp.clip(1.0 + 0.1 * jax.random.normal(seeds[3], (LAYERS, D), jnp.float32), 0.5, 1.5).astype(jnp.bfloat16)
    ln1_bias = normal_values(seeds[4], (LAYERS, D), 0.5, 3.0, ((1, 32),))
    qkv_weight = normal_values(seeds[5], (LAYERS, D, 3 * D), D ** -0.5, 0.21875, ((1, 32),))
    qv_bias = normal_values(seeds[6], (LAYERS, 2 * D), 0.5, 3.0, ((1, 32),))
    out_weight = normal_values(seeds[7], (LAYERS, D, D), (D // 64) ** -0.5, 1.75, ((1, 32),))
    out_bias = normal_values(seeds[8], (LAYERS, D), 0.5, 3.0, ((1, 32),))
    ln2_gain = jnp.clip(1.0 + 0.1 * jax.random.normal(seeds[9], (LAYERS, D), jnp.float32), 0.5, 1.5).astype(jnp.bfloat16)
    ln2_bias = normal_values(seeds[10], (LAYERS, D), 0.5, 3.0, ((1, 32),))
    fc_weight = normal_values(seeds[11], (LAYERS, D, FF), D ** -0.5, 0.21875, ((1, 32),))
    fc_bias = normal_values(seeds[12], (LAYERS, FF), 0.5, 3.0, ((1, 32),))
    proj_weight = normal_values(seeds[13], (LAYERS, FF, D), FF ** -0.5, 0.109375, ((1, 32),))
    proj_bias = normal_values(seeds[14], (LAYERS, D), 0.5, 3.0, ((1, 32),))
    return {"tokens": tokens, "cotangent": cotangent, "seq_len": seq_len, "ln1_gain": ln1_gain, "ln1_bias": ln1_bias, "qkv_weight": qkv_weight, "qv_bias": qv_bias, "out_weight": out_weight, "out_bias": out_bias, "ln2_gain": ln2_gain, "ln2_bias": ln2_bias, "fc_weight": fc_weight, "fc_bias": fc_bias, "proj_weight": proj_weight, "proj_bias": proj_bias}


@jax.custom_vjp
def low(v):
    return lax.optimization_barrier(v.astype(jnp.bfloat16)).astype(jnp.float32)

@jax.custom_vjp
def low_back(v):
    return v

def low_keep(v):
    return (low(v), None)

def low_pass(kept, grad):
    return (grad,)

def back_keep(v):
    return (v, None)

def back_low(kept, grad):
    return (low(grad),)
low.defvjp(low_keep, low_pass)
low_back.defvjp(back_keep, back_low)
eps = 1e-05

def both_round(value):
    return low(low_back(value))

def matmul(left, right):
    return jnp.dot(left, right, precision=lax.Precision.HIGHEST, preferred_element_type=jnp.float32)

def norm_rows(rows, gain, shift):
    mean = lax.optimization_barrier(jnp.mean(rows, axis=-1, keepdims=True))
    centred = rows - mean
    var = lax.optimization_barrier(jnp.mean(centred * centred, axis=-1, keepdims=True))
    return centred * lax.rsqrt(var + eps) * gain + shift

def one_layer(state, params, lengths):
    ln1_g, ln1_b, w_qkv, b_qv, w_out, b_out, ln2_g, ln2_b, w_fc, b_fc, w_proj, b_proj = params
    groups = lengths.shape[0]
    normed = low(norm_rows(state, ln1_g, ln1_b))
    qkv = matmul(normed, w_qkv)
    query = both_round(qkv[:, :D] + b_qv[:D]).reshape(groups, SEQ, H, HD)
    keys = both_round(qkv[:, D:2 * D]).reshape(groups, SEQ, H, HD)
    values = both_round(qkv[:, 2 * D:] + b_qv[D:]).reshape(groups, SEQ, H, HD)
    scores = jnp.einsum('gqhd,gkhd->ghqk', query, keys, precision=lax.Precision.HIGHEST) * (1.0 / math.sqrt(HD))
    scores = low_back(scores)
    place = jnp.arange(SEQ, dtype=jnp.int32)
    allowed = (place[None, None, :] <= place[None, :, None]) & (place[None, None, :] < lengths[:, None, None])
    scores = jnp.where(allowed[:, None], scores, -1e+30)
    top = lax.optimization_barrier(jnp.max(scores, axis=-1, keepdims=True))
    expo = jnp.exp(scores - top)
    probs = expo / lax.optimization_barrier(jnp.sum(expo, axis=-1, keepdims=True))
    attended = jnp.einsum('ghqk,gkhd->gqhd', low(probs), values, precision=lax.Precision.HIGHEST)
    attended = both_round(attended.reshape(groups * SEQ, D))
    branch = low_back(matmul(attended, w_out) + b_out)
    middle = state + branch
    normed2 = low(norm_rows(middle, ln2_g, ln2_b))
    pre = low_back(matmul(normed2, w_fc) + b_fc)
    act = low(jax.nn.gelu(pre, approximate=True))
    mlp = low_back(matmul(act, w_proj) + b_proj)
    return middle + mlp

def forward(inputs, params, lengths):
    place = jnp.arange(SEQ, dtype=jnp.int32)
    live = (place[None, :] < lengths[:, None]).reshape(-1, 1).astype(inputs.dtype)
    state = inputs
    for layer_index in range(LAYERS):
        state = one_layer(state, tuple((p[layer_index] for p in params)), lengths)
    return state * live

def reference(tokens, cotangent, seq_len, ln1_gain, ln1_bias, qkv_weight, qv_bias, out_weight, out_bias, ln2_gain, ln2_bias, fc_weight, fc_bias, proj_weight, proj_bias):
    params = tuple((p.astype(jnp.float32) for p in (ln1_gain, ln1_bias, qkv_weight, qv_bias, out_weight, out_bias, ln2_gain, ln2_bias, fc_weight, fc_bias, proj_weight, proj_bias)))
    groups = math.gcd(SLOTS, 8)
    count = SLOTS // groups
    inputs = tokens.astype(jnp.float32).reshape(count, groups * SEQ, D)
    cots = cotangent.astype(jnp.float32).reshape(count, groups * SEQ, D)
    lens = seq_len.reshape(count, groups)

    def step(totals, item):
        rows, cot_rows, lengths = item
        result, pull = jax.vjp(lambda a, b: forward(a, b, lengths), rows, params)
        grad_rows, grad_params = pull(cot_rows)
        totals = jax.tree.map(jnp.add, totals, grad_params)
        return (totals, (result.astype(jnp.bfloat16), grad_rows.astype(jnp.bfloat16)))
    zeros = tuple((jnp.zeros(p.shape, jnp.float32) for p in params))
    grads, (results, grad_in) = lax.scan(step, zeros, (inputs, cots, lens))
    return (results.reshape(TOKENS, D), grad_in.reshape(TOKENS, D), grads[0], grads[1], grads[2], grads[3], grads[4], grads[5], grads[6], grads[7], grads[8], grads[9], grads[10], grads[11])
```

```python
import math

import jax
import jax.numpy as jnp
from jax import lax
from jax.experimental import pallas as pl
from jax.experimental.pallas import tpu as pltpu
from jax.sharding import PartitionSpec as P

D = 768
HD = 64
SEQ = 512
LAYERS = 2


eps = 1e-05


def norm_stats(rows):
    mean = jnp.mean(rows, axis=-1, keepdims=True)
    centred = rows - mean
    var = jnp.mean(centred * centred, axis=-1, keepdims=True)
    inverse = lax.rsqrt(var + eps)
    return (centred * inverse, inverse)


def norm_back(grad_hat, hat, inverse):
    first = jnp.mean(grad_hat, axis=-1, keepdims=True)
    second = jnp.mean(grad_hat * hat, axis=-1, keepdims=True)
    return inverse * (grad_hat - first - hat * second)


def block_probs(query, keys, allowed):
    scores = lax.dot_general(
        query, keys, (((1,), (1,)), ((), ())), preferred_element_type=jnp.float32
    ) * (1.0 / math.sqrt(HD))
    scores = jnp.where(allowed, scores, -1e30)
    top = jnp.max(scores, axis=-1, keepdims=True)
    expo = jnp.exp(scores - top)
    return expo * (1.0 / jnp.sum(expo, axis=-1, keepdims=True))


def block_allowed(first, count, seen, length):
    row = lax.broadcasted_iota(jnp.int32, (count, seen), 0) + first
    column = lax.broadcasted_iota(jnp.int32, (count, seen), 1)
    return (column <= row) & (column < length)


def attend_kernel(length_ref, query_ref, keys_ref, values_ref, out_ref):
    length = length_ref[pl.program_id(0)]
    half = SEQ // 2
    for part in range(2):
        first, seen = part * half, (part + 1) * half
        rows = pl.ds(first, half)
        allowed = block_allowed(first, half, seen, length)
        for head in range(128 // HD):
            lanes = pl.ds(head * HD, HD)
            probs = block_probs(query_ref[rows, lanes], keys_ref[pl.ds(0, seen), lanes], allowed)
            attended = jnp.dot(
                probs.astype(jnp.bfloat16),
                values_ref[pl.ds(0, seen), lanes],
                preferred_element_type=jnp.float32,
            )
            out_ref[rows, lanes] = attended.astype(jnp.bfloat16)


def attend_back_kernel(
    length_ref, query_ref, keys_ref, values_ref, grad_ref, dq_ref, dk_ref, dv_ref
):
    length = length_ref[pl.program_id(0)]
    half = SEQ // 2
    scale = 1.0 / math.sqrt(HD)
    over_rows = (((0,), (0,)), ((), ()))
    for head in range(128 // HD):
        lanes = pl.ds(head * HD, HD)
        sums = []
        for part in range(2):
            first, seen = part * half, (part + 1) * half
            rows = pl.ds(first, half)
            keys = keys_ref[pl.ds(0, seen), lanes]
            query = query_ref[rows, lanes]
            grad = grad_ref[rows, lanes]
            allowed = block_allowed(first, half, seen, length)
            probs = block_probs(query, keys, allowed)
            dprob = lax.dot_general(
                grad,
                values_ref[pl.ds(0, seen), lanes],
                (((1,), (1,)), ((), ())),
                preferred_element_type=jnp.float32,
            )
            delta = jnp.sum(probs * dprob, axis=-1, keepdims=True)
            dscores = (probs * (dprob - delta)).astype(jnp.bfloat16)
            dq = jnp.dot(dscores, keys, preferred_element_type=jnp.float32) * scale
            dq_ref[rows, lanes] = dq.astype(jnp.bfloat16)
            dk = lax.dot_general(dscores, query, over_rows, preferred_element_type=jnp.float32)
            dv = lax.dot_general(
                probs.astype(jnp.bfloat16), grad, over_rows, preferred_element_type=jnp.float32
            )
            sums.append((dk, dv))
        low, high = pl.ds(0, half), pl.ds(half, half)
        (dk0, dv0), (dk1, dv1) = sums
        dk_ref[low, lanes] = ((dk0 + dk1[:half]) * scale).astype(jnp.bfloat16)
        dk_ref[high, lanes] = (dk1[half:] * scale).astype(jnp.bfloat16)
        dv_ref[low, lanes] = (dv0 + dv1[:half]).astype(jnp.bfloat16)
        dv_ref[high, lanes] = dv1[half:].astype(jnp.bfloat16)


def pair_block(offset):
    return pl.BlockSpec((SEQ, 128), lambda slot, pair: (slot, pair + offset))


def attend(qkv, lengths):
    pairs = D // 128
    return pl.pallas_call(
        attend_kernel,
        grid=(lengths.shape[0], pairs),
        in_specs=[pl.BlockSpec(memory_space=pltpu.SMEM)]
        + [pair_block(pairs * kind) for kind in range(3)],
        out_specs=pair_block(0),
        out_shape=jax.ShapeDtypeStruct((qkv.shape[0], D), jnp.bfloat16),
        compiler_params=pltpu.CompilerParams(vmem_limit_bytes=48 * 2**20),
        name="attend",
    )(lengths, qkv, qkv, qkv)


def attend_back(qkv, grad_att, lengths):
    pairs = D // 128
    shape = jax.ShapeDtypeStruct((qkv.shape[0], D), jnp.bfloat16)
    return pl.pallas_call(
        attend_back_kernel,
        grid=(lengths.shape[0], pairs),
        in_specs=[pl.BlockSpec(memory_space=pltpu.SMEM)]
        + [pair_block(pairs * kind) for kind in range(3)]
        + [pair_block(0)],
        out_specs=[pair_block(0)] * 3,
        out_shape=[shape] * 3,
        compiler_params=pltpu.CompilerParams(vmem_limit_bytes=48 * 2**20),
        name="attend_back",
    )(lengths, qkv, qkv, qkv, grad_att)


def forward_layer(state, weights, lengths):
    ln1_g, ln1_b, w_qkv, b_qv, w_out, b_out, ln2_g, ln2_b, w_fc, b_fc, w_proj, b_proj = weights
    hat1, inverse1 = norm_stats(state)
    normed = (hat1 * ln1_g + ln1_b).astype(jnp.bfloat16)
    qkv = jnp.dot(normed, w_qkv, preferred_element_type=jnp.float32)
    zeros = jnp.zeros((D,), b_qv.dtype)
    qkv = (qkv + jnp.concatenate([b_qv[:D], zeros, b_qv[D:]])).astype(jnp.bfloat16)
    attended = attend(qkv, lengths)
    middle = state + jnp.dot(attended, w_out, preferred_element_type=jnp.float32) + b_out
    hat2, inverse2 = norm_stats(middle)
    normed2 = (hat2 * ln2_g + ln2_b).astype(jnp.bfloat16)
    pre = jnp.dot(normed2, w_fc, preferred_element_type=jnp.float32) + b_fc
    act = jax.nn.gelu(pre, approximate=True).astype(jnp.bfloat16)
    result = middle + jnp.dot(act, w_proj, preferred_element_type=jnp.float32) + b_proj
    kept = (
        hat1,
        inverse1,
        normed,
        qkv,
        attended,
        hat2,
        inverse2,
        normed2,
        pre,
        act,
    )
    return (result, kept)


def column_sums(matrix):
    return jnp.sum(matrix.astype(jnp.float32), axis=0)


def backward_layer(grad, weights, kept, lengths):
    ln1_g, ln1_b, w_qkv, b_qv, w_out, b_out, ln2_g, ln2_b, w_fc, b_fc, w_proj, b_proj = weights
    (
        hat1,
        inverse1,
        normed,
        qkv,
        attended,
        hat2,
        inverse2,
        normed2,
        pre,
        act,
    ) = kept
    grad_mlp = grad.astype(jnp.bfloat16)
    g_proj_w = jnp.einsum("rf,rd->fd", act, grad_mlp, preferred_element_type=jnp.float32)
    g_proj_b = column_sums(grad_mlp)
    grad_act = jnp.einsum("rd,fd->rf", grad_mlp, w_proj, preferred_element_type=jnp.float32)
    _, gelu_pull = jax.vjp(lambda value: jax.nn.gelu(value, approximate=True), pre)
    grad_pre = gelu_pull(grad_act)[0].astype(jnp.bfloat16)
    g_fc_w = jnp.einsum("rd,rf->df", normed2, grad_pre, preferred_element_type=jnp.float32)
    g_fc_b = column_sums(grad_pre)
    grad_n2 = jnp.einsum("rf,df->rd", grad_pre, w_fc, preferred_element_type=jnp.float32)
    g_ln2_g = jnp.sum(grad_n2 * hat2, axis=0)
    g_ln2_b = jnp.sum(grad_n2, axis=0)
    grad_mid = grad + norm_back(grad_n2 * ln2_g, hat2, inverse2)
    grad_branch = grad_mid.astype(jnp.bfloat16)
    g_out_w = jnp.einsum("rc,rd->cd", attended, grad_branch, preferred_element_type=jnp.float32)
    g_out_b = column_sums(grad_branch)
    grad_att = jnp.einsum(
        "rd,cd->rc", grad_branch, w_out, preferred_element_type=jnp.float32
    ).astype(jnp.bfloat16)
    grad_q, grad_k, grad_v = attend_back(qkv, grad_att, lengths)
    grad_qkv = jnp.concatenate([grad_q, grad_k, grad_v], axis=1)
    g_qkv_w = jnp.einsum("rd,rc->dc", normed, grad_qkv, preferred_element_type=jnp.float32)
    g_qv_b = jnp.concatenate([column_sums(grad_q), column_sums(grad_v)])
    grad_n1 = jnp.einsum("rc,dc->rd", grad_qkv, w_qkv, preferred_element_type=jnp.float32)
    g_ln1_g = jnp.sum(grad_n1 * hat1, axis=0)
    g_ln1_b = jnp.sum(grad_n1, axis=0)
    grad_in = grad_mid + norm_back(grad_n1 * ln1_g, hat1, inverse1)
    grads = (
        g_ln1_g,
        g_ln1_b,
        g_qkv_w,
        g_qv_b,
        g_out_w,
        g_out_b,
        g_ln2_g,
        g_ln2_b,
        g_fc_w,
        g_fc_b,
        g_proj_w,
        g_proj_b,
    )
    return (grad_in, grads)


WIDTHS = (1, 1, 3 * D, 2, D, 1, 1, 1, 4 * D, 4, 4 * D, 1)


def pack(members, rows):
    wide = [member.reshape(rows, -1).astype(jnp.bfloat16) for member in members]
    large = [member for member in wide if member.shape[1] >= 128]
    small = jnp.concatenate([member for member in wide if member.shape[1] < 128], axis=1)
    small = jnp.pad(small, ((0, 0), (0, 128 - small.shape[1])))
    return jnp.concatenate(large + [small], axis=1)


def unpack(packed):
    large, small = 0, sum(width for width in WIDTHS if width >= 128)
    pieces = []
    for width in WIDTHS:
        if width >= 128:
            pieces.append(packed[:, large : large + width])
            large = large + width
        else:
            pieces.append(packed[:, small : small + width])
            small = small + width
    return pieces


def fetch(members):
    rows = members[0].shape[0]
    whole = lax.all_gather(pack(members, rows), "dp", axis=0, tiled=True)
    shapes = [(-1,) + member.shape[1:] for member in members]
    return tuple(piece.reshape(shape) for piece, shape in zip(unpack(whole), shapes))


def reduce_to_owners(grads, earlier):
    packed = pack(grads, D)
    if earlier is not None:
        packed, earlier = lax.optimization_barrier((packed, earlier))
    return lax.psum_scatter(packed, "dp", scatter_dimension=0, tiled=True), earlier


def shares_of(mine, shards):
    return [
        piece.astype(jnp.float32).reshape(shard.shape)
        for piece, shard in zip(unpack(mine), shards)
    ]


def body(tokens, cotangent, seq_len, *params):
    place = jnp.arange(SEQ, dtype=jnp.int32)
    live = (place[None, :] < seq_len[:, None]).reshape(-1, 1).astype(jnp.float32)
    shards = [tuple(member[index] for member in params) for index in range(LAYERS)]
    weights = [fetch(members) for members in shards]
    state = tokens.astype(jnp.float32)
    kept_all = []
    for index in range(LAYERS):
        state, kept = forward_layer(state, weights[index], seq_len)
        kept_all.append(kept)
    output = (state * live).astype(jnp.bfloat16)
    grad = cotangent.astype(jnp.float32) * live
    mine = [None] * (LAYERS + 1)
    for index in reversed(range(LAYERS)):
        grad, grads = backward_layer(grad, weights[index], kept_all[index], seq_len)
        mine[index], mine[index + 1] = reduce_to_owners(grads, mine[index + 1])
    layer_grads = [shares_of(mine[index], shards[index]) for index in range(LAYERS)]
    stacked = tuple(
        jnp.stack([layer_grads[index][member] for index in range(LAYERS)]) for member in range(12)
    )
    return (output, grad.astype(jnp.bfloat16)) + stacked


def solution(mesh):
    placed = (
        P("dp", None),
        P("dp", None),
        P("dp"),
        P(None, "dp"),
        P(None, "dp"),
        P(None, "dp", None),
        P(None, "dp"),
        P(None, "dp", None),
        P(None, "dp"),
        P(None, "dp"),
        P(None, "dp"),
        P(None, "dp", None),
        P(None, "dp"),
        P(None, "dp", None),
        P(None, "dp"),
    )
    return jax.shard_map(
        body,
        mesh=mesh,
        in_specs=placed,
        out_specs=(
            P("dp", None),
            P("dp", None),
            P(None, "dp"),
            P(None, "dp"),
            P(None, "dp", None),
            P(None, "dp"),
            P(None, "dp", None),
            P(None, "dp"),
            P(None, "dp"),
            P(None, "dp"),
            P(None, "dp", None),
            P(None, "dp"),
            P(None, "dp", None),
            P(None, "dp"),
        ),
        check_vma=False,
    )
```
